32 devices in a mesh: groups: 2 (over y), mp: 8 (over z, x), hidden: 2 (over core).
Axes of the slice: x: 2, y: 2, z: 4, core: 2. Of those that a mesh axis runs over, the one named last changes fastest.
Arguments:
- tokens: bfloat16 [48, 8192], P(('groups', 'mp'), 'hidden'), parts along dimension 0, may hold values from -6 to 6
- gate_weight: bfloat16 [8192, 2, 13312], P('hidden', None, 'mp'), may hold values from -0.0625 to 0.0625
- up_weight: bfloat16 [8192, 2, 13312], P('hidden', None, 'mp'), may hold values from -0.0625 to 0.0625
- down_weight: bfloat16 [2, 13312, 8192], P('hidden', None, 'mp'), may hold values from -0.0390625 to 0.0390625
Outputs:
- mixed: bfloat16 [48, 8192], P(('groups', 'hidden'), 'mp'), parts along dimension 0
The draws below stay inside these ranges and needn't reach their ends.
There are 2 independent parts, one for each index of `groups`. The reference program is written for one: setup_inputs(seed, part) draws one part's arguments, and reference() takes and returns one part's arrays. A program takes and returns all parts, laid end to end along the dimension named above; an argument that names none is the same for every part. Nothing has to cross between parts.
All inputs are finite; a program needn't handle non-finite values.
Results may differ from the reference program's by a relative error of at most 0.0049.
Values may be sent and summed in bfloat16 or wider, within the bound.
A program may use at most 192 MiB of HBM per device.

```python
import jax
import jax.numpy as jnp

D = 8192
FF = 26624
BANKS = 2
HALF = 13312
TOKENS = 24


def shard_levels(own_key, dims, split, least, high):
    def one(axis_at, blocks):
        heights = jax.random.uniform(jax.random.fold_in(jax.random.fold_in(own_key, 6), axis_at), (blocks,), jnp.float32, least / len(split), high / len(split))
        return jnp.repeat(jnp.exp(heights), dims[axis_at] // blocks).reshape((-1,) + (1,) * (len(dims) - axis_at - 1))

    factor_of = one(*split[0])
    for cut in split[1:]:
        factor_of = factor_of * one(*cut)
    return factor_of


def bell_draw(own_key, extent, scale, most, cuts=(), held_as=jnp.bfloat16):
    drawn = jax.random.normal(own_key, extent, jnp.float32) * scale
    if len(cuts) > 0:
        drawn = shard_levels(own_key, extent, cuts, -0.22, 0.18) * drawn
    return jnp.clip(drawn, min=-most, max=most).astype(held_as)


def setup_inputs(seed: int = 0, part: int = 0) -> dict:
    splits = jax.random.split(jax.random.key(seed), 5)
    part_keys = jax.random.split(jax.random.fold_in(splits[4], part), 5)
    tokens = bell_draw(part_keys[0], (TOKENS, D), 1.0, 6.0, ((0, 8), (1, 2)))
    gate_weight = bell_draw(splits[1], (D, BANKS, HALF), D ** -0.5, 0.0625, ((0, 2), (2, 8)))
    up_weight = bell_draw(splits[2], (D, BANKS, HALF), D ** -0.5, 0.0625, ((0, 2), (2, 8)))
    down_weight = bell_draw(splits[3], (BANKS, HALF, D), FF ** -0.5, 0.0390625, ((0, 2), (2, 8)))
    return dict(tokens=tokens, gate_weight=gate_weight, up_weight=up_weight, down_weight=down_weight)


def reference(tokens, gate_weight, up_weight, down_weight):
    gate = jnp.dot(tokens, gate_weight.reshape(D, FF), preferred_element_type=jnp.float32)
    up = jnp.dot(tokens, up_weight.reshape(D, FF), preferred_element_type=jnp.float32)
    act = (jax.nn.silu(gate) * up).astype(jnp.bfloat16)
    mixed = jnp.dot(act, down_weight.reshape(FF, D), preferred_element_type=jnp.float32)
    return mixed.astype(jnp.bfloat16)
```

```python
import functools

import jax
import jax.numpy as jnp
from jax import lax
from jax.experimental import pallas as pl
from jax.experimental.pallas import tpu as pltpu
from jax.sharding import PartitionSpec as P

MESH = pl.DeviceIdType.MESH
ROWS = 512
SLOTS = 5
VMEM_BYTES = 60 * 2**20


def kernel(
    n, cuts, x_ref, g_ref, u_ref, d_ref, o_ref,
    wbuf, dbuf, tok, xs, xe, acc, part, act, oacc, obuf, orecv,
    wsem, dsem, tsend, trecv, psend, precv, asend, arecv, osem,
):
    me = lax.axis_index("mp")
    half = lax.axis_index("hidden")
    other = 1 - half
    rows, width = x_ref.shape
    total, cols = act.shape[1:]
    steps = width // ROWS

    def peer(s):
        return lax.rem(me + s, n)

    def weight_copies(c, k, slot):
        f0, fc = cuts[c]
        start = pl.multiple_of(k * ROWS, ROWS)
        return [
            pltpu.make_async_copy(
                ref.at[pl.ds(start, ROWS), :, pl.ds(f0, fc)],
                wbuf.at[slot, i, :, :, pl.ds(0, fc)],
                wsem.at[slot, i],
            )
            for i, ref in enumerate((g_ref, u_ref))
        ]

    def weight_start(c, k):
        for copy in weight_copies(c, k, lax.rem(c * steps + k, SLOTS)):
            copy.start()

    def down_copy(c, s):
        f0, fc = cuts[c]
        p = peer(s)
        window = pl.ds(pl.multiple_of(p * cols + f0, 128), fc)
        return pltpu.make_async_copy(d_ref.at[0, window], dbuf.at[window], dsem.at[c, s])

    for k in range(SLOTS):
        weight_start(0, k)

    barrier = pltpu.get_barrier_semaphore()
    for s in range(1, n):
        pl.semaphore_signal(barrier, inc=1, device_id={"mp": peer(s)}, device_id_type=MESH)
    pl.semaphore_signal(barrier, inc=1, device_id={"hidden": other}, device_id_type=MESH)
    pl.semaphore_wait(barrier, n)

    def token_copy(s, slot):
        return pltpu.make_async_remote_copy(
            src_ref=x_ref, dst_ref=tok.at[slot], send_sem=tsend.at[s], recv_sem=trecv.at[slot],
            device_id={"mp": peer(s)}, device_id_type=MESH,
        )

    for s in range(1, n):
        token_copy(s, me).start()
    tok[me] = x_ref[...]
    for s in range(1, n):
        token_copy(s, peer(s)).wait_recv()
    for p in range(n):
        xs[pl.ds(p * rows, rows), :] = tok[p].astype(jnp.float32)

    place = lax.broadcasted_iota(jnp.int32, (128, 512), 0)
    spot = lax.broadcasted_iota(jnp.int32, (128, 512), 1)
    bank = spot // 256
    spread = jnp.where(2 * place + bank == spot - 256 * bank, 1.0, 0.0).astype(jnp.bfloat16)
    for j in range(width // 128):
        both = jnp.dot(
            xs[:, j * 128 : (j + 1) * 128].astype(jnp.bfloat16), spread,
            preferred_element_type=jnp.float32,
        )
        both = jnp.concatenate([both[:, :256], both[:, 256:]], axis=0)
        xe[:, j * 256 : (j + 1) * 256] = both.astype(jnp.bfloat16)

    def part_copy(c):
        f0, fc = cuts[c]
        return pltpu.make_async_remote_copy(
            src_ref=acc.at[:, other, :, pl.ds(f0, fc)], dst_ref=part.at[:, :, pl.ds(f0, fc)],
            send_sem=psend.at[c], recv_sem=precv.at[c],
            device_id={"hidden": other}, device_id_type=MESH,
        )

    def act_copy(c, s, slot):
        f0, fc = cuts[c]
        ref = act.at[slot, :, pl.ds(f0, fc)]
        return pltpu.make_async_remote_copy(
            src_ref=ref, dst_ref=ref, send_sem=asend.at[c, s], recv_sem=arecv.at[c, slot],
            device_id={"mp": peer(s)}, device_id_type=MESH,
        )

    def activate(c):
        f0, fc = cuts[c]
        part_copy(c).wait_recv()
        window = pl.ds(f0, fc)
        gate = acc[0, half, :, window] + part[0, :, window]
        up = acc[1, half, :, window] + part[1, :, window]
        act[me, :, window] = (gate / (1.0 + jnp.exp(-gate)) * up).astype(jnp.bfloat16)
        for s in range(1, n):
            act_copy(c, s, me).start()

    last = len(cuts) - 1
    for c, (f0, fc) in enumerate(cuts):
        window = pl.ds(f0, fc)
        acc[:, :, :, window] = jnp.zeros((2, 2, total, fc), jnp.float32)

        def step(k, carry, c=c, fc=fc, window=window):
            slot = lax.rem(c * steps + k, SLOTS)
            x = xe[:, pl.ds(pl.multiple_of(k * 2 * ROWS, 2 * ROWS), 2 * ROWS)]
            for i, copy in enumerate(weight_copies(c, k, slot)):
                copy.wait()
                w = wbuf[slot, i, :, :, pl.ds(0, fc)].reshape(2 * ROWS, fc)
                sums = jnp.dot(x, w, preferred_element_type=jnp.float32)
                acc[i, :, :, window] += sums.reshape(2, total, fc)
            ahead = k + SLOTS

            @pl.when(ahead < steps)
            def _():
                weight_start(c, ahead)

            if c < last:

                @pl.when(ahead >= steps)
                def _():
                    weight_start(c + 1, ahead - steps)

            else:
                for j in range(n // 2):

                    @pl.when(ahead - steps == j)
                    def _():
                        down_copy(0, 2 * j).start()
                        down_copy(0, 2 * j + 1).start()

            if c > 0:

                @pl.when(k == 1)
                def _():
                    activate(c - 1)

            return carry

        lax.fori_loop(0, steps, step, 0)
        part_copy(c).start()

    for c in range(1, len(cuts)):
        for s in range(n):
            down_copy(c, s).start()

    oacc[...] = jnp.zeros_like(oacc)

    def down(c, s):
        f0, fc = cuts[c]
        p = peer(s)
        if s > 0:
            act_copy(c, s, p).wait_recv()
        down_copy(c, s).wait()
        oacc[...] += jnp.dot(
            act[p, :, pl.ds(f0, fc)], dbuf[pl.ds(pl.multiple_of(p * cols + f0, 128), fc), :],
            preferred_element_type=jnp.float32,
        )

    for c in range(last):
        for s in range(n):
            if c == 0 and s == 3:
                activate(last)
            down(c, s)
    for s in range(n):
        down(last, s)

    own = total // 2
    obuf[0] = oacc[:own, :]
    obuf[1] = oacc[own:, :]
    swap = pltpu.make_async_remote_copy(
        src_ref=obuf.at[other], dst_ref=orecv, send_sem=osem.at[0], recv_sem=osem.at[1],
        device_id={"hidden": other}, device_id_type=MESH,
    )
    swap.start()
    swap.wait_recv()
    o_ref[...] = (obuf[half] + orecv[...]).astype(jnp.bfloat16)

    swap.wait_send()
    for s in range(1, n):
        token_copy(s, me).wait_send()
    for c in range(len(cuts)):
        part_copy(c).wait_send()
        for s in range(1, n):
            act_copy(c, s, me).wait_send()


def fused(n, tokens, gate_weight, up_weight, down_weight):
    rows, width = tokens.shape
    cols = gate_weight.shape[2]
    model = down_weight.shape[2]
    total = n * rows
    blocks = cols // 128
    first = (blocks + 1) // 2 * 128
    cuts = ((0, first), (first, cols - first))
    vmem, dma = pltpu.VMEM, pltpu.SemaphoreType.DMA
    in_vmem = pl.BlockSpec(memory_space=pltpu.VMEM)
    in_hbm = pl.BlockSpec(memory_space=pl.ANY)
    f32, bf16 = jnp.float32, jnp.bfloat16
    weights = gate_weight.size + up_weight.size + down_weight.size
    return pl.pallas_call(
        functools.partial(kernel, n, cuts),
        out_shape=jax.ShapeDtypeStruct((total // 2, model), bf16),
        in_specs=[in_vmem, in_hbm, in_hbm, in_hbm],
        out_specs=in_vmem,
        scratch_shapes=[
            vmem((SLOTS, 2, ROWS, 2, first), bf16),
            vmem((n * cols, model), bf16),
            vmem((n, rows, width), bf16),
            vmem((total, width), f32),
            vmem((2 * total, 2 * width), bf16),
            vmem((2, 2, total, cols), f32),
            vmem((2, total, cols), f32),
            vmem((n, total, cols), bf16),
            vmem((total, model), f32),
            vmem((2, total // 2, model), f32),
            vmem((total // 2, model), f32),
            dma((SLOTS, 2)),
            dma((2, n)),
            dma((n,)),
            dma((n,)),
            dma((2,)),
            dma((2,)),
            dma((2, n)),
            dma((2, n)),
            dma((2,)),
        ],
        compiler_params=pltpu.CompilerParams(
            collective_id=0, has_side_effects=True, vmem_limit_bytes=VMEM_BYTES
        ),
        cost_estimate=pl.CostEstimate(
            flops=2 * total * weights, bytes_accessed=2 * weights,
            transcendentals=total * cols,
        ),
    )(tokens, gate_weight, up_weight, down_weight)


def projector(gate_part, up_part, piece):
    gate = jnp.einsum("td,dbf->tbf", piece, gate_part, preferred_element_type=jnp.float32)
    up = jnp.einsum("td,dbf->tbf", piece, up_part, preferred_element_type=jnp.float32)
    return jnp.stack([gate, up])


def down_adder(weights, piece):
    return jnp.einsum("tbn,bnd->td", piece, weights, preferred_element_type=jnp.float32)


def plain(tokens, gate_weight, up_weight, down_weight):
    partial_sums = projector(
        gate_weight, up_weight, lax.all_gather(tokens, "mp", axis=0, tiled=True)
    )
    summed = lax.psum_scatter(partial_sums, "hidden", scatter_dimension=2, tiled=True)
    activation = (jax.nn.silu(summed[0]) * summed[1]).astype(jnp.bfloat16)
    partial_out = down_adder(down_weight, lax.all_gather(activation, "mp", axis=2, tiled=True))
    mixed = lax.psum_scatter(partial_out, "hidden", scatter_dimension=0, tiled=True)
    return mixed.astype(jnp.bfloat16)


def fits(n, tokens, gate_weight, down_weight):
    rows, width = tokens.shape
    banks, cols = gate_weight.shape[1:]
    total = n * rows
    return (
        banks == 2
        and n % 2 == 0
        and n >= 4
        and total % 8 == 0
        and total <= 64
        and cols % 128 == 0
        and cols >= 256
        and down_weight.shape[2] % 128 == 0
        and width % ROWS == 0
        and width // ROWS >= SLOTS >= n // 2
        and SLOTS * ROWS * 8 * (cols + 128) // 2 + down_weight.size * 2 < 52 * 2**20
    )


def solution(mesh):
    n = mesh.shape["mp"]

    def shards(tokens, gate_weight, up_weight, down_weight):
        if mesh.shape["hidden"] == 2 and fits(n, tokens, gate_weight, down_weight):
            return fused(n, tokens, gate_weight, up_weight, down_weight)
        return plain(tokens, gate_weight, up_weight, down_weight)

    in_specs = (
        P(("groups", "mp"), "hidden"),
        P("hidden", None, "mp"),
        P("hidden", None, "mp"),
        P("hidden", None, "mp"),
    )
    out_specs = P(("groups", "hidden"), "mp")
    return jax.shard_map(shards, mesh=mesh, in_specs=in_specs, out_specs=out_specs, check_vma=False)
```

```python
import functools

import jax
import jax.numpy as jnp
from jax import lax
from jax.experimental import pallas as pl
from jax.experimental.pallas import tpu as pltpu
from jax.sharding import PartitionSpec as P

MESH = pl.DeviceIdType.MESH
ROWS = 512
SLOTS = 5
VMEM_BYTES = 60 * 2**20


def kernel(
    n, cuts, x_ref, g_ref, u_ref, d_ref, o_ref,
    wbuf, dbuf, tok, xs, xe, acc, part, act, oacc, obuf, orecv,
    wsem, dsem, tsend, trecv, psend, precv, asend, arecv, osem,
):
    me = lax.axis_index("mp")
    half = lax.axis_index("hidden")
    other = 1 - half
    rows, width = x_ref.shape
    total, cols = act.shape[1:]
    steps = width // ROWS

    hops = n // 2
    beside = me + 1 - 2 * lax.rem(me, 2)

    def along(s):
        return lax.rem(me + 2 * s, n)

    def owner(s):
        if s <= 1:
            return (me, beside)[s]
        return along(s - 1) if s <= hops else lax.rem(beside + 2 * (s - hops), n)

    def direct(ref, ssem, rsem, j):
        return pltpu.make_async_remote_copy(
            src_ref=ref(me), dst_ref=ref(me), send_sem=ssem(j), recv_sem=rsem(me),
            device_id={"mp": along(j) if j else beside}, device_id_type=MESH,
        )

    def onward(ref, ssem, rsem, j):
        slot = along(j)
        return pltpu.make_async_remote_copy(
            src_ref=ref(slot), dst_ref=ref(slot), send_sem=ssem(hops + j), recv_sem=rsem(slot),
            device_id={"mp": beside}, device_id_type=MESH,
        )

    def arrived(ref, ssem, rsem, slot):
        pltpu.make_async_remote_copy(
            src_ref=ref(slot), dst_ref=ref(slot), send_sem=ssem(0), recv_sem=rsem(slot),
            device_id={"mp": beside}, device_id_type=MESH,
        ).wait_recv()

    def send(*gather):
        for j in (*range(1, hops), 0):
            direct(*gather, j).start()

    def pass_on(*gather):
        for j in range(1, hops):
            arrived(*gather, along(j))
            onward(*gather, j).start()

    def sent(*gather):
        for j in range(hops):
            direct(*gather, j).wait_send()
        for j in range(1, hops):
            onward(*gather, j).wait_send()

    def weight_copies(c, k, slot):
        f0, fc = cuts[c]
        start = pl.multiple_of(k * ROWS, ROWS)
        return [
            pltpu.make_async_copy(
                ref.at[pl.ds(start, ROWS), :, pl.ds(f0, fc)],
                wbuf.at[slot, i, :, :, pl.ds(0, fc)],
                wsem.at[slot, i],
            )
            for i, ref in enumerate((g_ref, u_ref))
        ]

    def weight_start(c, k):
        for copy in weight_copies(c, k, lax.rem(c * steps + k, SLOTS)):
            copy.start()

    def down_copy(c, s):
        f0, fc = cuts[c]
        p = owner(s)
        window = pl.ds(pl.multiple_of(p * cols + f0, 128), fc)
        return pltpu.make_async_copy(d_ref.at[0, window], dbuf.at[window], dsem.at[c, s])

    for k in range(SLOTS):
        weight_start(0, k)

    barrier = pltpu.get_barrier_semaphore()
    def peer(s):
        return lax.rem(me + s, n)

    for s in range(1, n):
        pl.semaphore_signal(barrier, inc=1, device_id={"mp": peer(s)}, device_id_type=MESH)
    pl.semaphore_signal(barrier, inc=1, device_id={"hidden": other}, device_id_type=MESH)
    pl.semaphore_wait(barrier, n)

    span = 2 * ROWS

    def token_copy(t, s, slot):
        window = pl.ds(pl.multiple_of(t * span, span), span)
        return pltpu.make_async_remote_copy(
            src_ref=x_ref.at[:, window], dst_ref=tok.at[slot, :, window],
            send_sem=tsend.at[t, s], recv_sem=trecv.at[t, slot],
            device_id={"mp": peer(s)}, device_id_type=MESH,
        )

    for t in range(steps // 2):
        for s in range(1, n):
            token_copy(t, s, me).start()
    tok[me] = x_ref[...]

    def prepare(t):
        for s in range(1, n):
            token_copy(t, s, peer(s)).wait_recv()
        for p in range(n):
            window = pl.ds(pl.multiple_of(t * span, span), span)
            xs[pl.ds(p * rows, rows), :] = tok[p, :, window].astype(jnp.float32)
        place = lax.broadcasted_iota(jnp.int32, (128, 512), 0)
        spot = lax.broadcasted_iota(jnp.int32, (128, 512), 1)
        bank = spot // 256
        spread = jnp.where(2 * place + bank == spot - 256 * bank, 1.0, 0.0).astype(jnp.bfloat16)
        for j in range(span // 128):
            both = jnp.dot(
                xs[:, j * 128 : (j + 1) * 128].astype(jnp.bfloat16), spread,
                preferred_element_type=jnp.float32,
            )
            both = jnp.concatenate([both[:, :256], both[:, 256:]], axis=0)
            start = pl.multiple_of(t * 2 * span + j * 256, 256)
            xe[:, pl.ds(start, 256)] = both.astype(jnp.bfloat16)

    def part_copy(c):
        f0, fc = cuts[c]
        return pltpu.make_async_remote_copy(
            src_ref=acc.at[:, other, :, pl.ds(f0, fc)], dst_ref=part.at[:, :, pl.ds(f0, fc)],
            send_sem=psend.at[c], recv_sem=precv.at[c],
            device_id={"hidden": other}, device_id_type=MESH,
        )

    def acts(c):
        f0, fc = cuts[c]
        return (
            lambda slot: act.at[slot, :, pl.ds(f0, fc)],
            lambda j: asend.at[c, j],
            lambda slot: arecv.at[c, slot],
        )

    def activate(c):
        f0, fc = cuts[c]
        part_copy(c).wait_recv()
        window = pl.ds(f0, fc)
        gate = acc[0, half, :, window] + part[0, :, window]
        up = acc[1, half, :, window] + part[1, :, window]
        act[me, :, window] = (gate / (1.0 + jnp.exp(-gate)) * up).astype(jnp.bfloat16)
        send(*acts(c))

    pieces = [(c, s) for c in range(len(cuts)) for s in range(n)]
    last = len(cuts) - 1
    for c, (f0, fc) in enumerate(cuts):
        window = pl.ds(f0, fc)
        acc[:, :, :, window] = jnp.zeros((2, 2, total, fc), jnp.float32)

        def step(k, carry, c=c, f0=f0, fc=fc):
            if c == 0:

                @pl.when(lax.rem(k, 2) == 0)
                def _():
                    prepare(k // 2)

            slot = lax.rem(c * steps + k, SLOTS)
            x = xe[:, pl.ds(pl.multiple_of(k * 2 * ROWS, 2 * ROWS), 2 * ROWS)]
            copies = weight_copies(c, k, slot)

            def block(i, at, wide):
                return wbuf[slot, i, :, :, pl.ds(at, wide)].reshape(2 * ROWS, wide)

            def add(i, at, sums):
                wide = sums.shape[1]
                acc[i, :, :, pl.ds(f0 + at, wide)] += sums.reshape(2, total, wide)

            rest = fc % 256
            for i in range(2):
                copies[i].wait()
                for at in range(0, fc - rest, 512):
                    wide = min(512, fc - rest - at)
                    add(i, at, jnp.dot(x, block(i, at, wide), preferred_element_type=jnp.float32))
            if rest:
                w = jnp.concatenate([block(0, fc - rest, rest), block(1, fc - rest, rest)], axis=1)
                sums = jnp.dot(x, w, preferred_element_type=jnp.float32)
                add(0, fc - rest, sums[:, :rest])
                add(1, fc - rest, sums[:, rest:])
            ahead = k + SLOTS

            @pl.when(ahead < steps)
            def _():
                weight_start(c, ahead)

            if c < last:

                @pl.when(ahead >= steps)
                def _():
                    weight_start(c + 1, ahead - steps)

            else:
                for j in range(SLOTS):

                    @pl.when(ahead - steps == j)
                    def _(j=j):
                        for piece in pieces[2 * j : 2 * j + 2]:
                            down_copy(*piece).start()

            if c > 0:

                @pl.when(k == 1)
                def _():
                    activate(c - 1)

                @pl.when(k == 5)
                def _():
                    pass_on(*acts(c - 1))

            return carry

        lax.fori_loop(0, steps, step, 0)
        part_copy(c).start()

    for piece in pieces[2 * SLOTS :]:
        down_copy(*piece).start()

    oacc[...] = jnp.zeros_like(oacc)

    def down(c, s):
        f0, fc = cuts[c]
        p = owner(s)
        if s == 1 or s > hops:
            arrived(*acts(c), p)
        down_copy(c, s).wait()
        oacc[...] += jnp.dot(
            act[p, :, pl.ds(f0, fc)], dbuf[pl.ds(pl.multiple_of(p * cols + f0, 128), fc), :],
            preferred_element_type=jnp.float32,
        )

    for c, s in pieces:
        if (c, s) == (0, 2):
            activate(last)
        if (c, s) == (last, 0):
            pass_on(*acts(last))
        down(c, s)

    own = total // 2
    obuf[0] = oacc[:own, :]
    obuf[1] = oacc[own:, :]
    swap = pltpu.make_async_remote_copy(
        src_ref=obuf.at[other], dst_ref=orecv, send_sem=osem.at[0], recv_sem=osem.at[1],
        device_id={"hidden": other}, device_id_type=MESH,
    )
    swap.start()
    swap.wait_recv()
    o_ref[...] = obuf[half] + orecv[...]

    swap.wait_send()
    for t in range(steps // 2):
        for s in range(1, n):
            token_copy(t, s, me).wait_send()
    for c in range(len(cuts)):
        part_copy(c).wait_send()
        sent(*acts(c))


def fused(n, tokens, gate_weight, up_weight, down_weight):
    rows, width = tokens.shape
    cols = gate_weight.shape[2]
    model = down_weight.shape[2]
    total = n * rows
    first = (cols // 128 * 13 // 20 + 1) // 2 * 256
    cuts = ((0, first), (first, cols - first))
    count = len(cuts)
    widest = max(fc for _, fc in cuts) // 128 // 2 * 256 + 128
    vmem, dma = pltpu.VMEM, pltpu.SemaphoreType.DMA
    in_vmem = pl.BlockSpec(memory_space=pltpu.VMEM)
    in_hbm = pl.BlockSpec(memory_space=pl.ANY)
    f32, bf16 = jnp.float32, jnp.bfloat16
    weights = gate_weight.size + up_weight.size + down_weight.size
    return pl.pallas_call(
        functools.partial(kernel, n, cuts),
        out_shape=jax.ShapeDtypeStruct((total // 2, model), f32),
        in_specs=[in_vmem, in_hbm, in_hbm, in_hbm],
        out_specs=in_vmem,
        scratch_shapes=[
            vmem((SLOTS, 2, ROWS, 2, widest), bf16),
            vmem((n * cols, model), bf16),
            vmem((n, rows, width), bf16),
            vmem((total, 2 * ROWS), f32),
            vmem((2 * total, 2 * width), bf16),
            vmem((2, 2, total, cols), f32),
            vmem((2, total, cols), f32),
            vmem((n, total, cols), bf16),
            vmem((total, model), f32),
            vmem((2, total // 2, model), f32),
            vmem((total // 2, model), f32),
            dma((SLOTS, 2)),
            dma((count, n)),
            dma((width // ROWS // 2, n)),
            dma((width // ROWS // 2, n)),
            dma((count,)),
            dma((count,)),
            dma((count, n)),
            dma((count, n)),
            dma((2,)),
        ],
        compiler_params=pltpu.CompilerParams(
            collective_id=0, has_side_effects=True, vmem_limit_bytes=VMEM_BYTES
        ),
        cost_estimate=pl.CostEstimate(
            flops=2 * total * weights, bytes_accessed=2 * weights,
            transcendentals=total * cols,
        ),
    )(tokens, gate_weight, up_weight, down_weight).astype(bf16)


def projector(gate_part, up_part, piece):
    gate = jnp.einsum("td,dbf->tbf", piece, gate_part, preferred_element_type=jnp.float32)
    up = jnp.einsum("td,dbf->tbf", piece, up_part, preferred_element_type=jnp.float32)
    return jnp.stack([gate, up])


def down_adder(weights, piece):
    return jnp.einsum("tbn,bnd->td", piece, weights, preferred_element_type=jnp.float32)


def plain(tokens, gate_weight, up_weight, down_weight):
    partial_sums = projector(
        gate_weight, up_weight, lax.all_gather(tokens, "mp", axis=0, tiled=True)
    )
    summed = lax.psum_scatter(partial_sums, "hidden", scatter_dimension=2, tiled=True)
    activation = (jax.nn.silu(summed[0]) * summed[1]).astype(jnp.bfloat16)
    partial_out = down_adder(down_weight, lax.all_gather(activation, "mp", axis=2, tiled=True))
    mixed = lax.psum_scatter(partial_out, "hidden", scatter_dimension=0, tiled=True)
    return mixed.astype(jnp.bfloat16)


def fits(n, tokens, gate_weight, down_weight):
    rows, width = tokens.shape
    banks, cols = gate_weight.shape[1:]
    total = n * rows
    return (
        banks == 2
        and n % 2 == 0
        and n >= 4
        and total % 8 == 0
        and total <= 64
        and cols % 128 == 0
        and cols >= 640
        and down_weight.shape[2] % 128 == 0
        and width % (2 * ROWS) == 0
        and width // ROWS >= SLOTS
        and width // ROWS > 5
        and SLOTS * ROWS * 8 * (cols * 13 // 20 + 256) + down_weight.size * 2 < 53 * 2**20
    )


def solution(mesh):
    n = mesh.shape["mp"]

    def shards(tokens, gate_weight, up_weight, down_weight):
        if mesh.shape["hidden"] == 2 and fits(n, tokens, gate_weight, down_weight):
            return fused(n, tokens, gate_weight, up_weight, down_weight)
        return plain(tokens, gate_weight, up_weight, down_weight)

    in_specs = (
        P(("groups", "mp"), "hidden"),
        P("hidden", None, "mp"),
        P("hidden", None, "mp"),
        P("hidden", None, "mp"),
    )
    out_specs = P(("groups", "hidden"), "mp")
    return jax.shard_map(shards, mesh=mesh, in_specs=in_specs, out_specs=out_specs, check_vma=False)
```
